32 devices in a mesh: dp: 8 (over z, x), tensor: 4 (over y, core).
Axes of the slice: x: 2, y: 2, z: 4, core: 2. Of those that a mesh axis runs over, the one named last changes fastest.
Arguments:
- query_rows: bfloat16 [16384, 8192], P('dp', 'tensor'), may hold values from -16 to 16
- key_rows: bfloat16 [16384, 1024], P('dp'), may hold values from -10 to 10
- value_rows: bfloat16 [16384, 1024], P('dp'), may hold values from -600 to 600
- segment_ids: int32 [16384], P('dp'), may hold values from 0 to 63, never falling along the last dimension, each value on 1 to 512 neighbouring positions
- norm_gain: float32 [8192], replicated, may hold values from 0.1 to 1.9
- draft_weight: bfloat16 [8192, 512], P('tensor', 'dp'), may hold values from -0.0625 to 0.0625
- targets: bfloat16 [16384, 512], P(('dp', 'tensor')), may hold values from -6 to 6
Outputs:
- grad_weight: float32 [8192, 512], P('tensor', 'dp')
The draws below stay inside these ranges and needn't reach their ends.
Inputs may be any that keep to these rules, and one draw needn't show every extreme that they name: `segment_ids`: document ids never fall along the tokens; a document has at most 512 tokens, and one has exactly 512.
All inputs are finite; a program needn't handle non-finite values.
Results may differ from the reference program's by a relative error of at most 0.0015.
Values may be sent and summed in bfloat16 or wider, within the bound.
A program may use at most 192 MiB of HBM per device.

```python
import math
import jax
import jax.numpy as jnp
import numpy as np
from jax import lax

D = 8192
HEADS = 64
KV_HEADS = 8
HEAD_DIM = 128
KEY_OUT = 512
SEQ = 2048
DOC_MAX = 512
TOKENS = 16384
DOCS = 64


def draw_key_rows(key, part):
    noise = jnp.clip(jax.random.normal(jax.random.fold_in(key, 1), (TOKENS, KV_HEADS * HEAD_DIM), jnp.float32), -6.0, 6.0)
    return noise.astype(jnp.bfloat16)


def draw_query_rows(key, part):
    noise = jnp.clip(jax.random.normal(jax.random.fold_in(key, 2), (TOKENS, HEADS * HEAD_DIM), jnp.float32), -6.0, 6.0)
    return noise.astype(jnp.bfloat16)


def draw_value_rows(key, part):
    columns = jnp.arange(KV_HEADS * HEAD_DIM)
    shared_of = (columns // HEAD_DIM).astype(jnp.float32)
    row_scale = jnp.exp(jax.random.uniform(jax.random.fold_in(key, 4), (TOKENS, 1), jnp.float32, 0.0, 2.302585))
    noise = jnp.clip(jax.random.normal(jax.random.fold_in(key, 3), (TOKENS, KV_HEADS * HEAD_DIM), jnp.float32), -6.0, 6.0)
    column_scale = 10.0 ** (shared_of / (KV_HEADS - 1))
    return (noise * column_scale[None, :] * row_scale).astype(jnp.bfloat16)


def level_of(stream_key, extent, split, low, high):
    def one(axis_at, blocks):
        draws = jax.random.uniform(jax.random.fold_in(jax.random.fold_in(stream_key, 6), axis_at), (blocks,), jnp.float32, low / len(split), high / len(split))
        return jnp.repeat(jnp.exp(draws), extent[axis_at] // blocks).reshape((-1,) + (1,) * (len(extent) - axis_at - 1))

    factor_of = one(*split[0])
    for cut in split[1:]:
        factor_of = factor_of * one(*cut)
    return factor_of


def split_up(number_of, total, reach, lean):
    weights = [(1 << 20) // math.isqrt(standing ** lean) + 1 for standing in range(2, number_of + 1)]
    surplus, counts = total - reach - (number_of - 1), [1] * (number_of - 1)
    while surplus > 0:
        movable = [i for i in range(number_of - 1) if counts[i] < reach]
        mass, left = sum([weights[i] for i in movable]), surplus
        for i in movable:
            more = min(reach - counts[i], max(1, left * weights[i] // mass), surplus)
            counts[i] = counts[i] + more
            surplus = surplus - more
    return np.array([reach] + counts)


def uneven_parts(own_key, count, total, bound, skew):
    if count == 2:
        one = jax.random.randint(own_key, (), max(1, total - bound), min(bound, total - 1) + 1)
        return jnp.stack([one, total - one])
    lengths = jnp.asarray(split_up(count, total, bound, skew), jnp.int32)
    pairs = (count - 1) // 2
    donor, taker = lengths[1:1 + 2 * pairs:2], lengths[2:2 + 2 * pairs:2]
    room = jnp.minimum(donor - 1, bound - taker)
    moved = jax.random.randint(jax.random.fold_in(own_key, 1), (pairs,), 0, 1 << 20) % (room + 1)
    lengths = lengths.at[1:1 + 2 * pairs:2].set(donor - moved).at[2:2 + 2 * pairs:2].set(taker + moved)
    return lengths[jax.random.permutation(jax.random.fold_in(own_key, 2), count)]


def normal_values(key, dims, spread, most, pieces=(), held_as=jnp.bfloat16):
    result = jax.random.normal(key, dims, jnp.float32) * spread
    if len(pieces) > 0:
        result = level_of(key, dims, pieces, -0.22, 0.18) * result
    return jnp.clip(result, min=-most, max=most).astype(held_as)


def setup_inputs(seed: int = 0) -> dict:
    seeds = jax.random.split(jax.random.key(seed), 8)
    return {
        "query_rows": draw_query_rows(jax.random.fold_in(seeds[7], 71), 0),
        "key_rows": draw_key_rows(jax.random.fold_in(seeds[7], 71), 0),
        "value_rows": draw_value_rows(jax.random.fold_in(seeds[7], 71), 0),
        "segment_ids": jnp.searchsorted(jnp.cumsum(uneven_parts(seeds[3], DOCS, TOKENS, DOC_MAX, 2)), jnp.arange(TOKENS), side="right").astype(jnp.int32),
        "norm_gain": jnp.clip(1.0 + 0.18 * jax.random.normal(seeds[4], (D,), jnp.float32), 0.1, 1.9),
        "draft_weight": normal_values(seeds[5], (D, KEY_OUT), D ** -0.5, 0.0625, ((0, 4), (1, 8))),
        "targets": normal_values(seeds[6], (TOKENS, KEY_OUT), 1.0, 6.0, ((0, 32),)),
    }


def attend_group(query_rows, key_rows, value_rows, segments):
    group = HEADS // KV_HEADS
    scale = HEAD_DIM ** (-0.5)
    length = query_rows.shape[0]
    places = jnp.arange(length, dtype=jnp.int32)
    allowed = (segments[:, None] == segments[None, :]) & (places[:, None] >= places[None, :])
    query_heads = query_rows.astype(jnp.float32).reshape(length, KV_HEADS, group, HEAD_DIM).transpose(1, 0, 2, 3)
    key_heads = key_rows.astype(jnp.float32).reshape(length, KV_HEADS, HEAD_DIM).transpose(1, 0, 2)
    value_heads = value_rows.astype(jnp.float32).reshape(length, KV_HEADS, HEAD_DIM).transpose(1, 0, 2)

    def one_head(operands):
        query_part, key_part, value_part = operands
        scores = jnp.einsum('qrd,kd->rqk', query_part, key_part) * scale
        scores = jnp.where(allowed[None], scores, -1e+30)
        shifted = jnp.exp(scores - lax.optimization_barrier(jnp.max(scores, axis=-1, keepdims=True)))
        probs = (shifted / lax.optimization_barrier(jnp.sum(shifted, axis=-1, keepdims=True))).astype(jnp.bfloat16)
        probs = lax.optimization_barrier(probs)
        mixed = jnp.einsum('rqk,kd->qrd', probs.astype(jnp.float32), value_part)
        return mixed.astype(jnp.bfloat16)
    outputs = lax.map(one_head, (query_heads, key_heads, value_heads))
    return outputs.transpose(1, 0, 2, 3).reshape(length, KV_HEADS * group * HEAD_DIM)

def reference(query_rows, key_rows, value_rows, segment_ids, norm_gain, draft_weight, targets):
    total_tokens = query_rows.shape[0]
    groups = total_tokens // SEQ

    def per_group(number):
        offset = number * SEQ
        return attend_group(lax.dynamic_slice_in_dim(query_rows, offset, SEQ, 0), lax.dynamic_slice_in_dim(key_rows, offset, SEQ, 0), lax.dynamic_slice_in_dim(value_rows, offset, SEQ, 0), lax.dynamic_slice_in_dim(segment_ids, offset, SEQ, 0))
    attended = lax.map(per_group, jnp.arange(groups, dtype=jnp.int32)).reshape(total_tokens, D)
    attended = lax.optimization_barrier(attended)
    features = attended.astype(jnp.float32)
    mean_square = lax.optimization_barrier(jnp.mean(features * features, axis=-1, keepdims=True))
    normed = (features * lax.rsqrt(mean_square + 1e-06) * norm_gain[None, :]).astype(jnp.bfloat16)
    predicted = jnp.dot(normed, draft_weight, preferred_element_type=jnp.float32)
    residual = predicted - targets.astype(jnp.float32)
    grad_pred = (jnp.clip(residual, -1.0, 1.0) / jnp.sqrt(jnp.float32(total_tokens))).astype(jnp.bfloat16)
    return jnp.dot(normed.T, grad_pred, preferred_element_type=jnp.float32)
```

```python
import functools

import jax
import jax.numpy as jnp
from jax import lax
from jax.experimental import pallas as pl
from jax.experimental.pallas import tpu as pltpu
from jax.sharding import PartitionSpec as P

D = 8192
HEADS = 64
KV_HEADS = 8
HEAD_DIM = 128
DOC_MAX = 512
BLOCK = 128
MIB = 1 << 20


def attend_kernel(heads, repeats, first_ref, start_ref, q_ref, k_ref, v_ref, segcol_ref, segrow_ref, o_ref, sq_ref):
    number = pl.program_id(0)
    low = start_ref[number]
    factor = HEAD_DIM ** (-0.5) * 1.4426950408889634
    stack = min(repeats, 4)

    def branch(blocks):
        span = blocks * BLOCK
        offset = pl.multiple_of((number - (blocks - 1)) * BLOCK, BLOCK)
        rows = lax.broadcasted_iota(jnp.int32, (BLOCK, span), 0) + (span - BLOCK)
        cols = lax.broadcasted_iota(jnp.int32, (BLOCK, span), 1)
        seg_k = jnp.concatenate(
            [segrow_ref[number - (blocks - 1) + j] for j in range(blocks)], axis=1
        )
        allowed = (segcol_ref[...] == seg_k) & (rows >= cols)
        bias = jnp.where(allowed, 0.0, -1e30).astype(jnp.float32)
        squares = jnp.zeros((BLOCK, HEAD_DIM), jnp.float32)
        for start in range(0, heads, stack):
            g = start // repeats
            keys = k_ref[pl.ds(offset, span), g * HEAD_DIM : (g + 1) * HEAD_DIM]
            values = v_ref[pl.ds(offset, span), g * HEAD_DIM : (g + 1) * HEAD_DIM]
            queries = jnp.concatenate(
                [q_ref[:, (start + r) * HEAD_DIM : (start + r + 1) * HEAD_DIM] for r in range(stack)],
                axis=0,
            )
            scores = lax.dot_general(
                queries, keys, (((1,), (1,)), ((), ())), preferred_element_type=jnp.float32
            ).reshape(stack, BLOCK, span) + bias[None]
            top = jnp.max(scores, axis=-1, keepdims=True)
            shifted = jnp.exp2((scores - top) * factor)
            total = jnp.sum(shifted, axis=-1, keepdims=True)
            probs = (shifted * (1.0 / total)).astype(jnp.bfloat16).reshape(stack * BLOCK, span)
            mixed = jnp.dot(probs, values, preferred_element_type=jnp.float32).astype(jnp.bfloat16)
            for r in range(stack):
                part = mixed[r * BLOCK : (r + 1) * BLOCK]
                o_ref[:, (start + r) * HEAD_DIM : (start + r + 1) * HEAD_DIM] = part
                wide = part.astype(jnp.float32)
                squares = squares + wide * wide
        sq_ref[0] = jnp.sum(squares.T, axis=0, keepdims=True)

    for blocks in range(1, DOC_MAX // BLOCK + 2):
        pl.when(number - low + 1 == blocks)(functools.partial(branch, blocks))


def attend(query_rows, key_rows, value_rows, segment_ids):
    length, width = query_rows.shape
    heads = width // HEAD_DIM
    group = HEADS // KV_HEADS
    head_count = max(1, heads // group)
    repeats = heads // head_count
    blocks = length // BLOCK
    first = (lax.axis_index("tensor") * heads // group) // head_count
    heads_of_block = segment_ids.reshape(blocks, BLOCK)[:, 0]
    starts = jnp.sum((segment_ids[None, :] < heads_of_block[:, None]).astype(jnp.int32), axis=1) // BLOCK
    kv_spec = pl.BlockSpec((length, head_count * HEAD_DIM), lambda i, f, s: (0, f[0]))
    return pl.pallas_call(
        functools.partial(attend_kernel, heads, repeats),
        out_shape=(
            jax.ShapeDtypeStruct((length, width), jnp.bfloat16),
            jax.ShapeDtypeStruct((blocks, 1, BLOCK), jnp.float32),
        ),
        grid_spec=pltpu.PrefetchScalarGridSpec(
            num_scalar_prefetch=2,
            grid=(blocks,),
            in_specs=[
                pl.BlockSpec((BLOCK, width), lambda i, f, s: (i, 0)),
                kv_spec,
                kv_spec,
                pl.BlockSpec((BLOCK, 1), lambda i, f, s: (i, 0)),
                pl.BlockSpec((blocks, 1, BLOCK), lambda i, f, s: (0, 0, 0)),
            ],
            out_specs=[
                pl.BlockSpec((BLOCK, width), lambda i, f, s: (i, 0)),
                pl.BlockSpec((1, 1, BLOCK), lambda i, f, s: (i, 0, 0)),
            ],
        ),
        compiler_params=pltpu.CompilerParams(vmem_limit_bytes=48 * MIB),
        cost_estimate=pl.CostEstimate(
            flops=4 * length * 512 * width, bytes_accessed=6 * length * width, transcendentals=length * 512 * heads
        ),
    )(
        jnp.reshape(first, (1,)).astype(jnp.int32),
        starts.astype(jnp.int32),
        query_rows,
        key_rows,
        value_rows,
        segment_ids.reshape(length, 1),
        segment_ids.reshape(blocks, 1, BLOCK),
    )


def loss_derivative(predicted, targets, total_tokens):
    residual = predicted - targets.astype(jnp.float32)
    return (jnp.clip(residual, -1.0, 1.0) / jnp.sqrt(jnp.float32(total_tokens))).astype(
        jnp.bfloat16
    )


def on_device(query_rows, key_rows, value_rows, segment_ids, norm_gain, draft_weight, targets):
    attended, squares = attend(query_rows, key_rows, value_rows, segment_ids)
    squares = squares.reshape(-1)
    length = query_rows.shape[0]
    total_tokens = length * lax.axis_size("dp")
    weight_slab = lax.all_gather(draft_weight, "dp", axis=1, tiled=True)
    slab_rows = weight_slab.shape[0]
    features = attended.astype(jnp.float32)
    summed = lax.psum(squares, "tensor")
    inverse = lax.rsqrt(summed / D + 1e-06)
    gain_part = lax.dynamic_slice_in_dim(
        norm_gain, lax.axis_index("tensor") * slab_rows, slab_rows, 0
    )
    normed = (features * inverse[:, None] * gain_part[None, :]).astype(jnp.bfloat16)
    predicted = lax.psum_scatter(
        jnp.dot(normed, weight_slab, preferred_element_type=jnp.float32),
        "tensor",
        scatter_dimension=0,
        tiled=True,
    )
    grad_pred = loss_derivative(predicted, targets, total_tokens)
    grad_slab = lax.dot_general(
        normed,
        lax.all_gather(grad_pred, "tensor", axis=0, tiled=True),
        (((0,), (0,)), ((), ())),
        preferred_element_type=jnp.float32,
    )
    return lax.psum_scatter(grad_slab, "dp", scatter_dimension=1, tiled=True)


def solution(mesh):
    placed = (
        P("dp", "tensor"),
        P("dp", None),
        P("dp", None),
        P("dp"),
        P(),
        P("tensor", "dp"),
        P(("dp", "tensor"), None),
    )
    return jax.shard_map(
        on_device, mesh=mesh, in_specs=placed, out_specs=P("tensor", "dp"), check_vma=False
    )
```

```python
import functools

import jax
import jax.numpy as jnp
from jax import lax
from jax.experimental import pallas as pl
from jax.experimental.pallas import tpu as pltpu
from jax.sharding import PartitionSpec as P

D = 8192
HEADS = 64
KV_HEADS = 8
HEAD_DIM = 128
DOC_MAX = 512
BLOCK = 128
MIB = 1 << 20


def attend_kernel(heads, repeats, first_ref, start_ref, q_ref, k_ref, v_ref, segcol_ref, segrow_ref, o_ref, sq_ref):
    number = pl.program_id(0)
    low = start_ref[number]
    factor = HEAD_DIM ** (-0.5) * 1.4426950408889634
    stack = min(repeats, 4)

    def branch(blocks):
        span = blocks * BLOCK
        offset = pl.multiple_of((number - (blocks - 1)) * BLOCK, BLOCK)
        rows = lax.broadcasted_iota(jnp.int32, (BLOCK, span), 0) + (span - BLOCK)
        cols = lax.broadcasted_iota(jnp.int32, (BLOCK, span), 1)
        seg_k = jnp.concatenate(
            [segrow_ref[number - (blocks - 1) + j] for j in range(blocks)], axis=1
        )
        allowed = (segcol_ref[...] == seg_k) & (rows >= cols)
        bias = jnp.where(allowed, 0.0, -1e30).astype(jnp.float32)
        squares = jnp.zeros((BLOCK, HEAD_DIM), jnp.float32)
        for start in range(0, heads, stack):
            g = start // repeats
            keys = k_ref[pl.ds(offset, span), g * HEAD_DIM : (g + 1) * HEAD_DIM]
            values = v_ref[pl.ds(offset, span), g * HEAD_DIM : (g + 1) * HEAD_DIM]
            queries = jnp.concatenate(
                [q_ref[:, (start + r) * HEAD_DIM : (start + r + 1) * HEAD_DIM] for r in range(stack)],
                axis=0,
            )
            scores = lax.dot_general(
                queries, keys, (((1,), (1,)), ((), ())), preferred_element_type=jnp.float32
            ).reshape(stack, BLOCK, span) + bias[None]
            top = jnp.max(scores, axis=-1, keepdims=True)
            shifted = jnp.exp2((scores - top) * factor)
            total = jnp.sum(shifted, axis=-1, keepdims=True)
            probs = (shifted * (1.0 / total)).astype(jnp.bfloat16).reshape(stack * BLOCK, span)
            mixed = jnp.dot(probs, values, preferred_element_type=jnp.float32).astype(jnp.bfloat16)
            for r in range(stack):
                part = mixed[r * BLOCK : (r + 1) * BLOCK]
                o_ref[:, (start + r) * HEAD_DIM : (start + r + 1) * HEAD_DIM] = part
                wide = part.astype(jnp.float32)
                squares = squares + wide * wide
        sq_ref[0] = jnp.sum(squares.T, axis=0, keepdims=True)

    for blocks in range(1, DOC_MAX // BLOCK + 2):
        pl.when(number - low + 1 == blocks)(functools.partial(branch, blocks))


def attend(query_rows, key_rows, value_rows, segment_ids):
    length, width = query_rows.shape
    heads = width // HEAD_DIM
    group = HEADS // KV_HEADS
    head_count = max(1, heads // group)
    repeats = heads // head_count
    blocks = length // BLOCK
    first = (lax.axis_index("tensor") * heads // group) // head_count
    heads_of_block = segment_ids.reshape(blocks, BLOCK)[:, 0]
    starts = jnp.sum((segment_ids[None, :] < heads_of_block[:, None]).astype(jnp.int32), axis=1) // BLOCK
    kv_spec = pl.BlockSpec((length, head_count * HEAD_DIM), lambda i, f, s: (0, f[0]))
    return pl.pallas_call(
        functools.partial(attend_kernel, heads, repeats),
        out_shape=(
            jax.ShapeDtypeStruct((length, width), jnp.bfloat16),
            jax.ShapeDtypeStruct((blocks, 1, BLOCK), jnp.float32),
        ),
        grid_spec=pltpu.PrefetchScalarGridSpec(
            num_scalar_prefetch=2,
            grid=(blocks,),
            in_specs=[
                pl.BlockSpec((BLOCK, width), lambda i, f, s: (i, 0)),
                kv_spec,
                kv_spec,
                pl.BlockSpec((BLOCK, 1), lambda i, f, s: (i, 0)),
                pl.BlockSpec((blocks, 1, BLOCK), lambda i, f, s: (0, 0, 0)),
            ],
            out_specs=[
                pl.BlockSpec((BLOCK, width), lambda i, f, s: (i, 0)),
                pl.BlockSpec((1, 1, BLOCK), lambda i, f, s: (i, 0, 0)),
            ],
        ),
        compiler_params=pltpu.CompilerParams(vmem_limit_bytes=48 * MIB),
        cost_estimate=pl.CostEstimate(
            flops=4 * length * 512 * width, bytes_accessed=6 * length * width, transcendentals=length * 512 * heads
        ),
    )(
        jnp.reshape(first, (1,)).astype(jnp.int32),
        starts.astype(jnp.int32),
        query_rows,
        key_rows,
        value_rows,
        segment_ids.reshape(length, 1),
        segment_ids.reshape(blocks, 1, BLOCK),
    )


def tail_kernel(
    teams, shards, x_hbm, w_hbm, sq_ref, gain_ref, target_ref, o_ref,
    x, w, sq_in, inverse, sib_out, sib_in, keep, far_in, slopes, acc, block, gx_out, gx_in, gz_out, gz_in,
    local_sem, sq_s, sq_r, sib_s, sib_r, far_s, far_r, own_s, pass_s, slope_r, gx_s, gx_r, gz_s, gz_r,
):
    me_t, me_d = lax.axis_index("tensor"), lax.axis_index("dp")
    pairs, lines = teams // 2, shards // 2
    k, c = me_t // 2, lax.rem(me_t, 2)
    h, p = me_d // 2, lax.rem(me_d, 2)
    length, width = x.shape
    part = length // teams
    piece = min(part, 256)
    columns = w.shape[1]
    own = columns // shards
    tokens = float(length * shards)
    chunk = min(width, 512)

    def copy(src, dst, send, recv, t=None, d=None):
        return pltpu.make_async_remote_copy(
            src_ref=src,
            dst_ref=dst,
            send_sem=send,
            recv_sem=recv,
            device_id=(me_d if d is None else d, me_t if t is None else t),
            device_id_type=pl.DeviceIdType.MESH,
        )

    load_x = pltpu.make_async_copy(x_hbm, x, local_sem.at[0])
    load_w = pltpu.make_async_copy(w_hbm, w, local_sem.at[1])
    load_x.start()
    load_w.start()

    barrier = pltpu.get_barrier_semaphore()
    for j in range(1, teams):
        pl.semaphore_signal(
            barrier, inc=1, device_id=(me_d, lax.rem(me_t + j, teams)), device_id_type=pl.DeviceIdType.MESH
        )
    for j in range(1, shards):
        pl.semaphore_signal(
            barrier, inc=1, device_id=(lax.rem(me_d + j, shards), me_t), device_id_type=pl.DeviceIdType.MESH
        )
    pl.semaphore_wait(barrier, teams + shards - 2)

    sent = []
    for j in range(1, teams):
        one = copy(sq_ref, sq_in.at[j], sq_s.at[j], sq_r.at[j], t=lax.rem(me_t + j, teams))
        one.start()
        sent.append(one)
    total = sq_ref[...]
    for j in range(1, teams):
        sent[j - 1].wait_recv()
        total = total + sq_in[j]
    inverse[...] = lax.rsqrt(total / D + 1e-06)
    load_x.wait()
    load_w.wait()

    def predict(owner, into):
        base = owner * part

        def norm(i, carry):
            rows = pl.ds(pl.multiple_of(base + i * BLOCK, BLOCK), BLOCK)
            row = inverse[pl.ds(owner * (part // BLOCK) + i, 1), :]
            column = jnp.broadcast_to(row, (BLOCK, BLOCK)).T[:, :1]
            x[rows, :] = (x[rows, :].astype(jnp.float32) * column * gain_ref[...]).astype(jnp.bfloat16)
            return carry

        lax.fori_loop(0, part // BLOCK, norm, 0)

        def multiply(i, carry):
            rows = pl.ds(pl.multiple_of(base + i * piece, BLOCK), piece)
            into[pl.ds(pl.multiple_of(i * piece, BLOCK), piece), :] = jnp.dot(
                x[rows, :], w[...], preferred_element_type=jnp.float32
            )
            return carry

        lax.fori_loop(0, part // piece, multiply, 0)

    arriving = {}
    for j in list(range(1, pairs)) + [0]:
        kk = lax.rem(k + j, pairs)
        predict(2 * kk + 1 - c, sib_out.at[j])
        one = copy(sib_out.at[j], sib_in.at[j], sib_s.at[j], sib_r.at[j], t=2 * k + 1 - c)
        one.start()
        sent.append(one)
        predict(2 * kk + c, keep.at[j])
        one.wait_recv()
        keep[j] = keep[j] + sib_in[j]
        if j:
            far = copy(keep.at[j], far_in.at[j], far_s.at[j], far_r.at[j], t=2 * kk + c)
            far.start()
            sent.append(far)
            arriving[j] = far
    for j in range(1, pairs):
        arriving[j].wait_recv()

    for i in range(part // BLOCK):
        rows = slice(i * BLOCK, (i + 1) * BLOCK)
        predicted = keep[0, rows, :]
        for j in range(1, pairs):
            predicted = predicted + far_in[j, rows, :]
        residual = predicted - target_ref[rows, :].astype(jnp.float32)
        slope = jnp.clip(residual, -1.0, 1.0) / jnp.sqrt(jnp.float32(tokens))
        slopes[me_t, :, rows] = slope.T.astype(jnp.bfloat16)

    for j in range(1, pairs):
        kk = lax.rem(k + j, pairs)
        one = copy(slopes.at[me_t], slopes.at[me_t], own_s.at[j], slope_r.at[me_t], t=2 * kk + c)
        one.start()
        sent.append(one)
    one = copy(slopes.at[me_t], slopes.at[me_t], own_s.at[0], slope_r.at[me_t], t=2 * k + 1 - c)
    one.start()
    sent.append(one)

    def arrived(slot):
        copy(slopes.at[slot], slopes.at[slot], own_s.at[0], slope_r.at[slot], t=2 * k + 1 - c).wait_recv()

    def product(owner, rows, cols):
        tokens_of = pl.ds(pl.multiple_of(owner * part, BLOCK), part)
        return jnp.dot(slopes[owner, rows, :], x[tokens_of, cols], preferred_element_type=jnp.float32)

    side = 2 * k + 1 - c
    arrived(side)

    def early(i, carry):
        cols = pl.ds(pl.multiple_of(i * chunk, BLOCK), chunk)
        for r in range(2):
            rows = slice(r * columns // 2, (r + 1) * columns // 2)
            acc[rows, cols] = product(me_t, rows, cols) + product(side, rows, cols)
        return carry

    lax.fori_loop(0, width // chunk, early, 0)
    for j in range(1, pairs):
        slot = 2 * lax.rem(k + pairs - j, pairs) + c
        arrived(slot)
        one = copy(slopes.at[slot], slopes.at[slot], pass_s.at[j], slope_r.at[slot], t=2 * k + 1 - c)
        one.start()
        sent.append(one)
    for j in range(1, pairs):
        arrived(2 * lax.rem(k + pairs - j, pairs) + 1 - c)

    crossing = {}
    for j in list(range(1, lines)) + [0]:
        hh = lax.rem(h + j, lines)
        rows = pl.ds(pl.multiple_of(hh * 2 * own, 2 * own), 2 * own)

        def late(i, carry):
            cols = pl.ds(pl.multiple_of(i * chunk, BLOCK), chunk)
            value = acc[rows, cols]
            for m in range(1, pairs):
                base = 2 * lax.rem(k + m, pairs)
                value = value + product(base, rows, cols) + product(base + 1, rows, cols)
            block[j, :, cols] = value
            return carry

        lax.fori_loop(0, width // chunk, late, 0)
        gx_out[j] = block[j, pl.ds(pl.multiple_of((1 - p) * own, own), own), :].astype(jnp.bfloat16)
        one = copy(gx_out.at[j], gx_in.at[j], gx_s.at[j], gx_r.at[j], d=2 * h + 1 - p)
        one.start()
        sent.append(one)
        crossing[j] = one

    mine = pl.ds(pl.multiple_of(p * own, own), own)
    landing = []
    for j in range(1, lines):
        hh = lax.rem(h + j, lines)
        crossing[j].wait_recv()
        gz_out[j] = block[j, mine, :] + gx_in[j].astype(jnp.float32)
        one = copy(gz_out.at[j], gz_in.at[j], gz_s.at[j], gz_r.at[j], d=2 * hh + p)
        one.start()
        sent.append(one)
        landing.append(one)
    crossing[0].wait_recv()
    o_ref[...] = block[0, mine, :] + gx_in[0].astype(jnp.float32)
    for j in range(1, lines):
        landing[j - 1].wait_recv()
        o_ref[...] += gz_in[j]
    for one in sent:
        one.wait_send()


def tail(attended, weight_slab, squares, gain_part, targets):
    teams, shards = lax.axis_size("tensor"), lax.axis_size("dp")
    length, width = attended.shape
    columns = weight_slab.shape[1]
    pairs, lines, part, own = teams // 2, shards // 2, length // teams, columns // shards
    vmem = pl.BlockSpec(memory_space=pltpu.VMEM)
    anywhere = pl.BlockSpec(memory_space=pl.ANY)
    f32, bf16 = jnp.float32, jnp.bfloat16
    dma = pltpu.SemaphoreType.DMA
    return pl.pallas_call(
        functools.partial(tail_kernel, teams, shards),
        out_shape=jax.ShapeDtypeStruct((own, width), f32),
        in_specs=[anywhere, anywhere, vmem, vmem, vmem],
        out_specs=vmem,
        scratch_shapes=[
            pltpu.VMEM((length, width), bf16),
            pltpu.VMEM((width, columns), bf16),
            pltpu.VMEM((teams,) + squares.shape, f32),
            pltpu.VMEM(squares.shape, f32),
            pltpu.VMEM((pairs, part, columns), f32),
            pltpu.VMEM((pairs, part, columns), f32),
            pltpu.VMEM((pairs, part, columns), f32),
            pltpu.VMEM((pairs, part, columns), f32),
            pltpu.VMEM((teams, columns, part), bf16),
            pltpu.VMEM((columns, width), f32),
            pltpu.VMEM((lines, 2 * own, width), f32),
            pltpu.VMEM((lines, own, width), bf16),
            pltpu.VMEM((lines, own, width), bf16),
            pltpu.VMEM((lines, own, width), f32),
            pltpu.VMEM((lines, own, width), f32),
            dma((2,)),
            dma((teams,)),
            dma((teams,)),
            dma((pairs,)),
            dma((pairs,)),
            dma((pairs,)),
            dma((pairs,)),
            dma((pairs,)),
            dma((pairs,)),
            dma((teams,)),
            dma((lines,)),
            dma((lines,)),
            dma((lines,)),
            dma((lines,)),
        ],
        compiler_params=pltpu.CompilerParams(
            collective_id=0, has_side_effects=True, vmem_limit_bytes=52 * MIB
        ),
        cost_estimate=pl.CostEstimate(
            flops=4 * length * width * columns, bytes_accessed=2 * length * width, transcendentals=0
        ),
    )(attended, weight_slab, squares, gain_part, targets)


def on_device(query_rows, key_rows, value_rows, segment_ids, norm_gain, draft_weight, targets):
    weight_slab = lax.all_gather(draft_weight, "dp", axis=1, tiled=True)
    slab_rows = weight_slab.shape[0]
    gain_part = lax.dynamic_slice_in_dim(
        norm_gain, lax.axis_index("tensor") * slab_rows, slab_rows, 0
    ).reshape(1, slab_rows)
    attended, squares = attend(query_rows, key_rows, value_rows, segment_ids)
    squares = squares.reshape(-1, BLOCK)
    return tail(attended, weight_slab, squares, gain_part, targets).T


def solution(mesh):
    placed = (
        P("dp", "tensor"),
        P("dp", None),
        P("dp", None),
        P("dp"),
        P(),
        P("tensor", "dp"),
        P(("dp", "tensor"), None),
    )
    return jax.shard_map(
        on_device, mesh=mesh, in_specs=placed, out_specs=P("tensor", "dp"), check_vma=False
    )
```
